32 devices in a mesh: groups: 2 (over x), inp: 8 (over z, y), out: 2 (over core).
Axes of the slice: x: 2, y: 2, z: 4, core: 2. Of those that a mesh axis runs over, the one named last changes fastest.
Arguments:
- inputs: bfloat16 [1024, 4096], P(('groups', 'inp'), 'out'), parts along dimension 0, may hold values from -6 to 6
- pre_act: bfloat16 [1024, 12288], P('groups', 'inp'), parts along dimension 0, may hold values from -6 to 6
- out_grad: bfloat16 [1024, 4096], P(('groups', 'inp'), 'out'), parts along dimension 0, may hold values from -0.15625 to 0.15625
- w_down: bfloat16 [12288, 4096], P('inp', 'out'), may hold values from -0.0546875 to 0.0546875
- gram_state: float32 [4096, 2, 2048], P(('groups', 'inp'), 'out'), parts along dimension 0, may hold values from -6 to 6
Outputs:
- grad_down: bfloat16 [24576, 4096], P(('groups', 'inp'), 'out'), parts along dimension 0
- grad_up: bfloat16 [8192, 12288], P(('groups', 'out'), 'inp'), parts along dimension 0
- gram_new: float32 [4096, 2, 2048], P(('groups', 'inp'), 'out'), parts along dimension 0
The draws below stay inside these ranges and needn't reach their ends.
There are 2 independent parts, one for each index of `groups`. The reference program is written for one: setup_inputs(seed, part) draws one part's arguments, and reference() takes and returns one part's arrays. A program takes and returns all parts, laid end to end along the dimension named above; an argument that names none is the same for every part. Nothing has to cross between parts.
All inputs are finite; a program needn't handle non-finite values.
Results may differ from the reference program's by a relative error of at most 0.008.
Values may be sent and summed in bfloat16 or wider, within the bound.
A program may use at most 128 MiB of HBM per device.

```python
import jax
import jax.numpy as jnp
from jax import lax

D = 4096
F = 12288
BLOCK = 2048
TOKENS = 512
NBLK = 2
N_INP = 8


def level_of(own_key, extent, cuts, low, largest):
    def one(axis_at, shards_of):
        draws = jax.random.uniform(jax.random.fold_in(jax.random.fold_in(own_key, 6), axis_at), (shards_of,), jnp.float32, low / len(cuts), largest / len(cuts))
        return jnp.repeat(jnp.exp(draws), extent[axis_at] // shards_of).reshape((-1,) + (1,) * (len(extent) - axis_at - 1))

    factor_of = one(*cuts[0])
    for cut in cuts[1:]:
        factor_of = factor_of * one(*cut)
    return factor_of


def normal_values(stream_key, dims, spread, reach, cuts=(), kind=jnp.bfloat16):
    loudness = level_of(stream_key, dims, cuts, -0.22, 0.18) if cuts else 1.0
    result = jax.random.normal(stream_key, dims, jnp.float32) * spread * loudness
    return jnp.minimum(jnp.maximum(result, -reach), reach).astype(kind)


def setup_inputs(seed: int = 0, part: int = 0) -> dict:
    key_of = jax.random.split(jax.random.key(seed), 6)
    part_keys = jax.random.split(jax.random.fold_in(key_of[5], part), 6)
    return {
        "inputs": normal_values(part_keys[0], (TOKENS, D), 1.0, 6.0, ((0, 8), (1, 2))),
        "pre_act": normal_values(part_keys[1], (TOKENS, F), 1.0, 6.0, ((1, 8),)),
        "out_grad": normal_values(part_keys[2], (TOKENS, D), (0.25 * TOKENS ** -0.5), 0.15625, ((0, 8), (1, 2))),
        "w_down": normal_values(key_of[3], (F, D), F ** -0.5, 0.0546875, ((0, 8), (1, 2))),
        "gram_state": normal_values(part_keys[4], (BLOCK, NBLK, BLOCK), 1.0, 6.0, ((0, 8), (1, 2)), jnp.float32),
    }


inv_root_two = 0.7071067811865476
inv_root_two_pi = 0.3989422804014327
ema_decay = 0.95


def gelu_pair(pre_float):
    normal_cdf = 0.5 * (1.0 + lax.erf(pre_float * inv_root_two))
    density = jnp.exp(-0.5 * pre_float * pre_float) * inv_root_two_pi
    return pre_float * normal_cdf, normal_cdf + pre_float * density


def reference(inputs, pre_act, out_grad, w_down, gram_state):
    gelu_value, gelu_slope = gelu_pair(pre_act.astype(jnp.float32))
    activation = gelu_value.astype(jnp.bfloat16)
    grad_down = jnp.dot(activation.T, out_grad, preferred_element_type=jnp.float32).astype(jnp.bfloat16)
    act_grad = jnp.dot(out_grad, w_down.T, preferred_element_type=jnp.float32)
    hid_grad = (act_grad * gelu_slope).astype(jnp.bfloat16)
    grad_up = jnp.dot(inputs.T, hid_grad, preferred_element_type=jnp.float32).astype(jnp.bfloat16)
    shards = grad_down.reshape(N_INP, F // N_INP, D // BLOCK, BLOCK)

    def shard_gram(total, shard):
        wide = shard.astype(jnp.float32)
        gram_term = jnp.einsum("fbj,fbc->jbc", wide, wide)
        rounded = lax.optimization_barrier(gram_term.astype(jnp.bfloat16))
        return total + rounded.astype(jnp.float32), None

    summed, _ = lax.scan(shard_gram, jnp.zeros((BLOCK, D // BLOCK, BLOCK), jnp.float32), shards)
    gram_new = ema_decay * gram_state + (1.0 - ema_decay) * summed
    return grad_down, grad_up, gram_new
```

```python
import jax
import jax.numpy as jnp
from jax import lax
from jax.sharding import PartitionSpec as P

inv_root_two = 0.7071067811865476
inv_root_two_pi = 0.3989422804014327
ema_decay = 0.95


def gelu_pair(pre_float):
    normal_cdf = 0.5 * (1.0 + lax.erf(pre_float * inv_root_two))
    density = jnp.exp(-0.5 * pre_float * pre_float) * inv_root_two_pi
    return (pre_float * normal_cdf, normal_cdf + pre_float * density)


def over_rows(left, right):
    return lax.dot_general(
        left, right, (((0,), (0,)), ((), ())), preferred_element_type=jnp.float32
    )


def over_columns(left, right):
    return lax.dot_general(
        left, right, (((1,), (1,)), ((), ())), preferred_element_type=jnp.float32
    )


def split_two(value):
    high = value.astype(jnp.bfloat16)
    return high, (value - high.astype(jnp.float32)).astype(jnp.bfloat16)


def shards(inputs, pre_act, out_grad, w_down, gram_state):
    gelu_value, gelu_slope = gelu_pair(pre_act.astype(jnp.float32))
    activation = gelu_value.astype(jnp.bfloat16)
    portion = lax.all_gather(out_grad, "inp", axis=0, tiled=True)
    token_gram = lax.psum(over_columns(activation, activation), "inp")
    product = over_columns(portion, w_down)
    act_grad = lax.psum(product, "out")
    down_sum = over_rows(activation, portion)
    grad_down = down_sum.astype(jnp.bfloat16)
    hid_grad = (act_grad * gelu_slope).astype(jnp.bfloat16)
    up_total = over_rows(lax.all_gather(inputs, "inp", axis=0, tiled=True), hid_grad)
    grad_up = up_total.astype(jnp.bfloat16)
    rows = gram_state.shape[0]
    own = lax.dynamic_slice_in_dim(portion, lax.axis_index("inp") * rows, rows, 1)
    gram_high, gram_low = split_two(token_gram)
    left_high, left_low = split_two(over_rows(own, gram_high) + over_rows(own, gram_low))
    summed = jnp.dot(left_high, portion, preferred_element_type=jnp.float32) + jnp.dot(
        left_low, portion, preferred_element_type=jnp.float32
    )
    gram_new = ema_decay * gram_state + (1.0 - ema_decay) * summed[:, None, :]
    return (grad_down, grad_up, gram_new)


def solution(mesh):
    return jax.shard_map(
        shards,
        mesh=mesh,
        in_specs=(
            P(("groups", "inp"), "out"),
            P("groups", "inp"),
            P(("groups", "inp"), "out"),
            P("inp", "out"),
            P(("groups", "inp"), "out", None),
        ),
        out_specs=(
            P(("groups", "inp"), "out"),
            P(("groups", "out"), "inp"),
            P(("groups", "inp"), "out", None),
        ),
        check_vma=False,
    )
```

```python
import functools

import jax
import jax.numpy as jnp
from jax import lax
from jax.experimental import pallas as pl
from jax.experimental.pallas import tpu as pltpu
from jax.sharding import PartitionSpec as P

inv_root_two = 0.7071067811865476
inv_root_two_pi = 0.3989422804014327
ema_decay = 0.95
MESH = pl.DeviceIdType.MESH
BF16 = jnp.bfloat16
F32 = jnp.float32
CHUNKS = 4


def gelu_pair(pre_float):
    normal_cdf = 0.5 * (1.0 + lax.erf(pre_float * inv_root_two))
    density = jnp.exp(-0.5 * pre_float * pre_float) * inv_root_two_pi
    return (pre_float * normal_cdf, normal_cdf + pre_float * density)


def nt(left, right):
    return lax.dot_general(left, right, (((1,), (1,)), ((), ())), preferred_element_type=F32)


def tn(left, right):
    return lax.dot_general(left, right, (((0,), (0,)), ((), ())), preferred_element_type=F32)


def nn(left, right):
    return jnp.dot(left, right, preferred_element_type=F32)


def exchange(
    n,
    inputs,
    pre_act,
    out_grad,
    w_down,
    o_full,
    i_full,
    hid_out,
    act_out,
    s_out,
    o_v,
    pre_v,
    act_v,
    act_t,
    w_v,
    slope_v,
    own_v,
    part_send,
    part_recv,
    hid_v,
    s1_keep,
    s1_send,
    s1_recv,
    s2_send,
    s2_recv,
    s_v,
    ring_send,
    ring_recv,
    part_ssem,
    part_rsem,
    s1_sem,
    s2_ssem,
    s2_rsem,
    s3_ssem,
    s3_rsem,
    s4_sem,
    s5_sem,
    pre_sem,
    local_sem,
):
    grp, idx, core = lax.axis_index("groups"), lax.axis_index("inp"), lax.axis_index("out")
    ts, width = out_grad.shape
    tokens, hidden = pre_act.shape
    half_rows = ts // 2
    A = n // 2
    a, b = lax.div(idx, 2), lax.rem(idx, 2)
    hops = n // 2
    folded = n <= 8

    def at(p):
        p = lax.rem(p + 2 * n, n)
        if not folded:
            return p
        q = lax.div(p, A)
        return (1 - q) * (2 * p) + q * (2 * (n - 1 - p) + 1)

    pos = a * (1 - b) + (n - 1 - a) * b if folded else idx

    def slot(i):
        return lax.rem(i, 2) * A + lax.div(i, 2)

    def dev(i, c=core):
        return (grp, i, c)

    barrier = pltpu.get_barrier_semaphore()
    for d in range(1, n):
        pl.semaphore_signal(barrier, inc=1, device_id=dev(lax.rem(idx + d, n)), device_id_type=MESH)
    pl.semaphore_signal(barrier, inc=1, device_id=dev(idx, 1 - core), device_id_type=MESH)

    w_copy = pltpu.make_async_copy(w_down, w_v, local_sem.at[0])
    w_copy.start()
    pre_copies = []
    for j in range(n):
        copy = pltpu.make_async_copy(
            pre_act.at[pl.ds(j * ts, ts)], pre_v.at[pl.ds(((j % 2) * A + j // 2) * ts, ts)], pre_sem.at[j]
        )
        copy.start()
        pre_copies.append(copy)
    own_rows = pl.ds(pl.multiple_of(slot(idx) * ts, ts), ts)
    o_own = pltpu.make_async_copy(out_grad, o_v.at[own_rows], local_sem.at[1])
    o_own.start()
    i_own = pltpu.make_async_copy(inputs, i_full.at[own_rows], local_sem.at[2])
    i_own.start()
    pl.semaphore_wait(barrier, n)

    arrays = ((out_grad, o_v), (inputs, i_full))

    def exists(way, h, half):
        return h < hops or half == way

    def message(arr, way, h, half):
        sign = 1 - 2 * way
        mine, full = arrays[arr]
        place = slot(at(pos - sign * (h - 1)))
        rows = pl.ds(pl.multiple_of(place * ts + half * half_rows, half_rows), half_rows)
        src = mine.at[pl.ds(half * half_rows, half_rows)] if h == 1 else full.at[rows]
        return pltpu.make_async_remote_copy(
            src_ref=src,
            dst_ref=full.at[rows],
            send_sem=ring_send.at[arr, way, h - 1, half],
            recv_sem=ring_recv.at[arr, way, h - 1, half],
            device_id=dev(at(pos + sign)),
            device_id_type=MESH,
        )

    def arrived(arr, way, h, half):
        sign = 1 - 2 * way
        full = arrays[arr][1]
        place = slot(at(pos - sign * h))
        rows = pl.ds(pl.multiple_of(place * ts + half * half_rows, half_rows), half_rows)
        return pltpu.make_async_remote_copy(
            src_ref=full.at[rows],
            dst_ref=full.at[rows],
            send_sem=ring_send.at[arr, way, h - 1, half],
            recv_sem=ring_recv.at[arr, way, h - 1, half],
            device_id=dev(at(pos + sign)),
            device_id_type=MESH,
        )

    sent = []

    def push(arr, h, half, ways=(0, 1)):
        for way in ways:
            if exists(way, h, half):
                copy = message(arr, way, h, half)
                copy.start()
                sent.append(copy)

    def tick(arr, h, half):
        for way in (0, 1):
            if exists(way, h, half):
                arrived(arr, way, h, half).wait_recv()
                if h < hops:
                    push(arr, h + 1, half, (way,))

    for half in (0, 1):
        push(0, 1, half)

    ticks = [(h, half) for h in range(1, hops + 1) for half in (0, 1)]
    col = 256 if hidden % 256 == 0 else 128
    gelu_rows = 32

    def gelu_part(j):
        pre_copies[(j // A) + 2 * (j % A)].wait()

        @pl.loop(0, ts // gelu_rows)
        def _(r):
            rows = pl.ds(pl.multiple_of(j * ts + r * gelu_rows, gelu_rows), gelu_rows)

            @pl.loop(0, hidden // col)
            def _(c):
                cols = pl.ds(pl.multiple_of(c * col, col), col)
                value, slope = gelu_pair(pre_v[rows, cols].astype(F32))
                act_v[rows, cols] = value.astype(BF16)
                slope_v[rows, cols] = slope

    for k, (h, half) in enumerate(ticks):
        if k < n:
            gelu_part(k)
        tick(0, h, half)
        if (h, half) == (max(hops - 2, 1), 1):
            for other in (0, 1):
                push(1, 1, other)
    for k in range(len(ticks), n):
        gelu_part(k)
    o_own.wait()
    o_store = pltpu.make_async_copy(o_v, o_full, local_sem.at[1])
    o_store.start()

    span = tokens // 2
    core_cols = pl.ds(pl.multiple_of(core * span, span), span)
    partner = 2 * a + 1 - b
    group_rows = A * ts

    def s_rows(parity, keep):
        @pl.loop(0, A)
        def _(k):
            rows = pl.ds(pl.multiple_of(parity * group_rows + k * ts, ts), ts)
            value = nt(act_v[rows, :], act_v[core_cols, :])
            if keep:
                s1_keep[k] = value
            else:
                s1_send[k] = value.astype(BF16)

    s_rows(1 - b, False)
    s1 = pltpu.make_async_remote_copy(
        src_ref=s1_send,
        dst_ref=s1_recv,
        send_sem=s1_sem.at[0],
        recv_sem=s1_sem.at[1],
        device_id=dev(partner),
        device_id_type=MESH,
    )
    s1.start()
    s_rows(b, True)

    i_ticks = list(ticks)

    def next_tick():
        if i_ticks:
            tick(1, *i_ticks.pop(0))

    w_copy.wait()
    part_rows = tokens // CHUNKS
    part_copies = []
    for k in range(CHUNKS):
        rows = pl.ds(k * part_rows, part_rows)
        wcol = 512 if hidden % 512 == 0 else 128

        @pl.loop(0, hidden // wcol)
        def _(c):
            cols = pl.ds(pl.multiple_of(c * wcol, wcol), wcol)
            value = nt(o_v[rows, :], w_v[cols, :])
            own_v[rows, cols] = value
            part_send[rows, cols] = value.astype(BF16)

        copy = pltpu.make_async_remote_copy(
            src_ref=part_send.at[rows],
            dst_ref=part_recv.at[rows],
            send_sem=part_ssem.at[k],
            recv_sem=part_rsem.at[k],
            device_id=dev(idx, 1 - core),
            device_id_type=MESH,
        )
        copy.start()
        part_copies.append(copy)
        next_tick()

    s1.wait()

    @pl.loop(0, A)
    def _(k):
        value = s1_keep[k] + s1_recv[k].astype(F32)
        s1_keep[k] = value
        s2_send[k] = value.astype(BF16)

    s2_copies = []
    for d in range(1, A):
        there = lax.rem(a + d, A)
        copy = pltpu.make_async_remote_copy(
            src_ref=s2_send.at[there],
            dst_ref=s2_recv.at[d - 1],
            send_sem=s2_ssem.at[d - 1],
            recv_sem=s2_rsem.at[d - 1],
            device_id=dev(2 * there + b),
            device_id_type=MESH,
        )
        copy.start()
        s2_copies.append(copy)

    for k in range(CHUNKS):
        part_copies[k].wait_recv()

        @pl.loop(0, part_rows // gelu_rows)
        def _(r):
            rows = pl.ds(pl.multiple_of(k * part_rows + r * gelu_rows, gelu_rows), gelu_rows)

            @pl.loop(0, hidden // col)
            def _(c):
                cols = pl.ds(pl.multiple_of(c * col, col), col)
                total = own_v[rows, cols] + part_recv[rows, cols].astype(F32)
                hid_v[rows, cols] = (total * slope_v[rows, cols]).astype(BF16)

        if k % 2 == 1:
            next_tick()
    hid_store = pltpu.make_async_copy(hid_v, hid_out, local_sem.at[3])
    hid_store.start()

    for copy in s2_copies:
        copy.wait()
    total = s1_keep[a]
    for d in range(A - 1):
        total = total + s2_recv[d].astype(F32)
    s_v[core, b, a] = total.astype(BF16)
    s3_copies = []
    for d in range(1, A):
        there = lax.rem(a + d, A)
        copy = pltpu.make_async_remote_copy(
            src_ref=s_v.at[core, b, a],
            dst_ref=s_v.at[core, b, a],
            send_sem=s3_ssem.at[d - 1],
            recv_sem=s3_rsem.at[d - 1],
            device_id=dev(2 * there + b),
            device_id_type=MESH,
        )
        copy.start()
        s3_copies.append(copy)

    @pl.loop(0, hidden // 128)
    def _(c):
        block = pl.ds(pl.multiple_of(c * 128, 128), 128)
        act_t[block, :] = act_v[:, block].T

    act_store = pltpu.make_async_copy(act_t, act_out, local_sem.at[0])
    act_store.start()
    for d in range(1, A):
        copy = s3_copies[d - 1]
        copy.wait_send()
        back = lax.rem(a - d + A, A)
        pltpu.make_async_remote_copy(
            src_ref=s_v.at[core, b, back],
            dst_ref=s_v.at[core, b, back],
            send_sem=s3_ssem.at[d - 1],
            recv_sem=s3_rsem.at[d - 1],
            device_id=dev(2 * back + b),
            device_id_type=MESH,
        ).wait_recv()

    def swap(mine, theirs, sems, device):
        copy = pltpu.make_async_remote_copy(
            src_ref=s_v.at[mine],
            dst_ref=s_v.at[mine],
            send_sem=sems.at[0],
            recv_sem=sems.at[1],
            device_id=device,
            device_id_type=MESH,
        )
        copy.start()
        back = pltpu.make_async_remote_copy(
            src_ref=s_v.at[theirs],
            dst_ref=s_v.at[theirs],
            send_sem=sems.at[0],
            recv_sem=sems.at[1],
            device_id=device,
            device_id_type=MESH,
        )
        return copy, back

    copy, back = swap((core, b), (core, 1 - b), s4_sem, dev(partner))
    next_tick()
    copy.wait_send()
    back.wait_recv()
    copy, back = swap((core,), (1 - core,), s5_sem, dev(idx, 1 - core))
    while i_ticks:
        next_tick()
    copy.wait_send()
    back.wait_recv()
    s_store = pltpu.make_async_copy(s_v, s_out, local_sem.at[4])
    s_store.start()
    for copy in sent:
        copy.wait_send()
    for copy in part_copies:
        copy.wait_send()
    i_own.wait()
    o_store.wait()
    hid_store.wait()
    act_store.wait()
    s_store.wait()


def finish(act_t, hid, o_tile, i_tile, own, s, state, down, up, gram, left, s_keep, g_keep, sem):
    step = pl.program_id(0)
    rows = own.shape[1]
    tile = o_tile.shape[1]
    cols = pl.ds(pl.multiple_of(step * tile, tile), tile)

    @pl.when(step == 0)
    def _():
        copy = pltpu.make_async_copy(state.at[:, 0, :], s_keep, sem.at[0])
        copy.start()
        span = s.shape[2]
        for c in range(2):
            value = tn(own[...], s[c])
            high = value.astype(BF16)
            left[0, :, c * span : (c + 1) * span] = high
            left[1, :, c * span : (c + 1) * span] = (value - high.astype(F32)).astype(BF16)
        copy.wait()

    down[...] = nn(act_t[...], o_tile[...]).astype(BF16)
    up[...] = tn(i_tile[...], hid[...]).astype(BF16)
    total = nn(left[0], o_tile[...]) + nn(left[1], o_tile[...])
    g_keep[:, cols] = ema_decay * s_keep[:, cols] + (1.0 - ema_decay) * total

    @pl.when(step == pl.num_programs(0) - 1)
    def _():
        copy = pltpu.make_async_copy(g_keep, gram.at[:, 0, :], sem.at[1])
        copy.start()
        copy.wait()


def shards(n, inputs, pre_act, out_grad, w_down, gram_state):
    ts, width = out_grad.shape
    tokens, hidden = pre_act.shape
    A = n // 2
    span = tokens // 2
    hops = n // 2
    shape = jax.ShapeDtypeStruct
    dma = pltpu.SemaphoreType.DMA
    any_spec = pl.BlockSpec(memory_space=pl.ANY)
    vmem_spec = pl.BlockSpec(memory_space=pltpu.VMEM)
    extra = max(A - 1, 1)
    o_full, i_full, hid, act_t, s = pl.pallas_call(
        functools.partial(exchange, n),
        out_shape=(
            shape((tokens, width), BF16),
            shape((tokens, width), BF16),
            shape((tokens, hidden), BF16),
            shape((hidden, tokens), BF16),
            shape((2, 2, A, ts, span), BF16),
        ),
        in_specs=[any_spec, any_spec, vmem_spec, any_spec],
        out_specs=(any_spec,) * 5,
        scratch_shapes=[
            pltpu.VMEM((tokens, width), BF16),
            pltpu.VMEM((tokens, hidden), BF16),
            pltpu.VMEM((tokens, hidden), BF16),
            pltpu.VMEM((hidden, tokens), BF16),
            pltpu.VMEM((hidden, width), BF16),
            pltpu.VMEM((tokens, hidden), F32),
            pltpu.VMEM((tokens, hidden), F32),
            pltpu.VMEM((tokens, hidden), BF16),
            pltpu.VMEM((tokens, hidden), BF16),
            pltpu.VMEM((tokens, hidden), BF16),
            pltpu.VMEM((A, ts, span), F32),
            pltpu.VMEM((A, ts, span), BF16),
            pltpu.VMEM((A, ts, span), BF16),
            pltpu.VMEM((A, ts, span), BF16),
            pltpu.VMEM((extra, ts, span), BF16),
            pltpu.VMEM((2, 2, A, ts, span), BF16),
            dma((2, 2, hops, 2)),
            dma((2, 2, hops, 2)),
            dma((CHUNKS,)),
            dma((CHUNKS,)),
            dma((2,)),
            dma((extra,)),
            dma((extra,)),
            dma((extra,)),
            dma((extra,)),
            dma((2,)),
            dma((2,)),
            dma((n,)),
            dma((5,)),
        ],
        compiler_params=pltpu.CompilerParams(
            collective_id=0, has_side_effects=True, vmem_limit_bytes=56 * 1024 * 1024
        ),
        name="exchange",
    )(inputs, pre_act, out_grad, w_down)
    s = s.reshape(2, tokens, span)
    rows = gram_state.shape[0]
    own = lax.dynamic_slice_in_dim(o_full, lax.axis_index("inp") * rows, rows, 1)
    tile = 256
    keep = lambda i: (0, 0)
    return pl.pallas_call(
        finish,
        grid=(width // tile,),
        out_shape=(
            shape((hidden, width), BF16),
            shape((width, hidden), BF16),
            shape(gram_state.shape, F32),
        ),
        in_specs=[
            pl.BlockSpec((hidden, tokens), keep),
            pl.BlockSpec((tokens, hidden), keep),
            pl.BlockSpec((tokens, tile), lambda i: (0, i)),
            pl.BlockSpec((tokens, tile), lambda i: (0, i)),
            pl.BlockSpec((tokens, rows), keep),
            pl.BlockSpec((2, tokens, span), lambda i: (0, 0, 0)),
            any_spec,
        ],
        out_specs=(
            pl.BlockSpec((hidden, tile), lambda i: (0, i)),
            pl.BlockSpec((tile, hidden), lambda i: (i, 0)),
            any_spec,
        ),
        scratch_shapes=[
            pltpu.VMEM((2, rows, tokens), BF16),
            pltpu.VMEM((rows, width), F32),
            pltpu.VMEM((rows, width), F32),
            dma((2,)),
        ],
        compiler_params=pltpu.CompilerParams(vmem_limit_bytes=56 * 1024 * 1024),
        name="finish",
    )(act_t, hid, o_full, i_full, own, s, gram_state)


def solution(mesh):
    return jax.shard_map(
        functools.partial(shards, mesh.shape["inp"]),
        mesh=mesh,
        in_specs=(
            P(("groups", "inp"), "out"),
            P("groups", "inp"),
            P(("groups", "inp"), "out"),
            P("inp", "out"),
            P(("groups", "inp"), "out", None),
        ),
        out_specs=(
            P(("groups", "inp"), "out"),
            P(("groups", "out"), "inp"),
            P(("groups", "inp"), "out", None),
        ),
        check_vma=False,
    )
```

```python
import functools

import jax
import jax.numpy as jnp
from jax import lax
from jax.experimental import pallas as pl
from jax.experimental.pallas import tpu as pltpu
from jax.sharding import PartitionSpec as P

inv_root_two = 0.7071067811865476
inv_root_two_pi = 0.3989422804014327
ema_decay = 0.95
MESH = pl.DeviceIdType.MESH
BF16 = jnp.bfloat16
STEPS = 4
F32 = jnp.float32


def gelu_pair(pre_float):
    normal_cdf = 0.5 * (1.0 + lax.erf(pre_float * inv_root_two))
    density = jnp.exp(-0.5 * pre_float * pre_float) * inv_root_two_pi
    return (pre_float * normal_cdf, normal_cdf + pre_float * density)


def nt(left, right):
    return lax.dot_general(left, right, (((1,), (1,)), ((), ())), preferred_element_type=F32)


def tn(left, right):
    return lax.dot_general(left, right, (((0,), (0,)), ((), ())), preferred_element_type=F32)


def nn(left, right):
    return jnp.dot(left, right, preferred_element_type=F32)


def exchange(
    n,
    inputs,
    pre_act,
    out_grad,
    w_down,
    o_full,
    i_full,
    hid_out,
    act_out,
    s_out,
    o_v,
    pre_v,
    act_v,
    act_t,
    w_v,
    slope_v,
    own_v,
    part_send,
    part_recv,
    hid_v,
    s1_keep,
    s1_send,
    s1_recv,
    s2_send,
    s2_recv,
    s_v,
    ring_send,
    ring_recv,
    part_ssem,
    part_rsem,
    s1_sem,
    s2_ssem,
    s2_rsem,
    s3_ssem,
    s3_rsem,
    s4_sem,
    s5_sem,
    pre_sem,
    hid_sem,
    local_sem,
):
    grp, idx, core = lax.axis_index("groups"), lax.axis_index("inp"), lax.axis_index("out")
    ts, width = out_grad.shape
    tokens, hidden = pre_act.shape
    half_rows = ts // 2
    A = n // 2
    a, b = lax.div(idx, 2), lax.rem(idx, 2)
    hops = n // 2
    folded = n <= 8

    def at(p):
        p = lax.rem(p + 2 * n, n)
        if not folded:
            return p
        q = lax.div(p, A)
        return (1 - q) * (2 * p) + q * (2 * (n - 1 - p) + 1)

    pos = a * (1 - b) + (n - 1 - a) * b if folded else idx

    def slot(i):
        return lax.rem(i, 2) * A + lax.div(i, 2)

    def dev(i, c=core):
        return (grp, i, c)

    barrier = pltpu.get_barrier_semaphore()
    for d in range(1, n):
        pl.semaphore_signal(barrier, inc=1, device_id=dev(lax.rem(idx + d, n)), device_id_type=MESH)
    pl.semaphore_signal(barrier, inc=1, device_id=dev(idx, 1 - core), device_id_type=MESH)

    w_copy = pltpu.make_async_copy(w_down, w_v, local_sem.at[0])
    w_copy.start()
    pre_copies = []
    for j in range(n):
        copy = pltpu.make_async_copy(
            pre_act.at[pl.ds(j * ts, ts)], pre_v.at[pl.ds(((j % 2) * A + j // 2) * ts, ts)], pre_sem.at[j]
        )
        copy.start()
        pre_copies.append(copy)
    own_rows = pl.ds(pl.multiple_of(slot(idx) * ts, ts), ts)
    o_own = pltpu.make_async_copy(out_grad, o_v.at[own_rows], local_sem.at[1])
    o_own.start()
    i_own = pltpu.make_async_copy(inputs, i_full.at[own_rows], local_sem.at[2])
    i_own.start()
    pl.semaphore_wait(barrier, n)

    arrays = ((out_grad, o_v), (inputs, i_full))

    def exists(way, h, half):
        return h < hops or half == way

    def message(arr, way, h, half):
        sign = 1 - 2 * way
        mine, full = arrays[arr]
        place = slot(at(pos - sign * (h - 1)))
        rows = pl.ds(pl.multiple_of(place * ts + half * half_rows, half_rows), half_rows)
        src = mine.at[pl.ds(half * half_rows, half_rows)] if h == 1 else full.at[rows]
        return pltpu.make_async_remote_copy(
            src_ref=src,
            dst_ref=full.at[rows],
            send_sem=ring_send.at[arr, way, h - 1, half],
            recv_sem=ring_recv.at[arr, way, h - 1, half],
            device_id=dev(at(pos + sign)),
            device_id_type=MESH,
        )

    def arrived(arr, way, h, half):
        sign = 1 - 2 * way
        full = arrays[arr][1]
        place = slot(at(pos - sign * h))
        rows = pl.ds(pl.multiple_of(place * ts + half * half_rows, half_rows), half_rows)
        return pltpu.make_async_remote_copy(
            src_ref=full.at[rows],
            dst_ref=full.at[rows],
            send_sem=ring_send.at[arr, way, h - 1, half],
            recv_sem=ring_recv.at[arr, way, h - 1, half],
            device_id=dev(at(pos + sign)),
            device_id_type=MESH,
        )

    sent = []

    def push(arr, h, half, ways=(0, 1)):
        for way in ways:
            if exists(way, h, half):
                copy = message(arr, way, h, half)
                copy.start()
                sent.append(copy)

    def tick(arr, h, half):
        for way in (0, 1):
            if exists(way, h, half):
                arrived(arr, way, h, half).wait_recv()
                if h < hops:
                    push(arr, h + 1, half, (way,))

    for half in (0, 1):
        push(0, 1, half)
        push(1, 1, half)

    def step(arr, h):
        for half in (0, 1):
            tick(arr, h, half)

    col = 256 if hidden % 256 == 0 else 128
    gelu_rows = 32

    def gelu_part(j):
        pre_copies[(j // A) + 2 * (j % A)].wait()

        @pl.loop(0, ts // gelu_rows)
        def _(r):
            rows = pl.ds(pl.multiple_of(j * ts + r * gelu_rows, gelu_rows), gelu_rows)

            @pl.loop(0, hidden // col)
            def _(c):
                cols = pl.ds(pl.multiple_of(c * col, col), col)
                value, slope = gelu_pair(pre_v[rows, cols].astype(F32))
                act_v[rows, cols] = value.astype(BF16)
                slope_v[rows, cols] = slope

    part_copies = []

    def shards_of(h):
        if h == 0:
            return [slot(idx)]
        if h == hops:
            return [slot(at(pos + h))]
        return [slot(at(pos - h)), slot(at(pos + h))]

    wcol = 512 if hidden % 512 == 0 else 128

    def part(h):
        for place in shards_of(h):
            rows = pl.ds(pl.multiple_of(place * ts, ts), ts)

            @pl.loop(0, hidden // wcol)
            def _(c):
                cols = pl.ds(pl.multiple_of(c * wcol, wcol), wcol)
                value = nt(o_v[rows, :], w_v[cols, :])
                own_v[rows, cols] = value
                part_send[rows, cols] = value.astype(BF16)

            k = len(part_copies)
            copy = pltpu.make_async_remote_copy(
                src_ref=part_send.at[rows],
                dst_ref=part_recv.at[rows],
                send_sem=part_ssem.at[k],
                recv_sem=part_rsem.at[k],
                device_id=dev(idx, 1 - core),
                device_id_type=MESH,
            )
            copy.start()
            part_copies.append(copy)

    hid_done = []
    hid_stores = []

    def hid_part(h):
        for place in shards_of(h):
            k = len(hid_done)
            hid_done.append(k)
            part_copies[k].wait_recv()

            @pl.loop(0, ts // gelu_rows)
            def _(r):
                start = place * ts + r * gelu_rows
                rows = pl.ds(pl.multiple_of(start, gelu_rows), gelu_rows)

                @pl.loop(0, hidden // col)
                def _(c):
                    cols = pl.ds(pl.multiple_of(c * col, col), col)
                    total = own_v[rows, cols] + part_recv[rows, cols].astype(F32)
                    hid_v[rows, cols] = (total * slope_v[rows, cols]).astype(BF16)

            rows = pl.ds(pl.multiple_of(place * ts, ts), ts)
            store = pltpu.make_async_copy(hid_v.at[rows], hid_out.at[rows], hid_sem.at[k])
            store.start()
            hid_stores.append(store)

    span = tokens // 2
    core_cols = pl.ds(pl.multiple_of(core * span, span), span)
    partner = 2 * a + 1 - b
    group_rows = A * ts

    def s_rows(parity, keep):
        @pl.loop(0, A)
        def _(k):
            rows = pl.ds(pl.multiple_of(parity * group_rows + k * ts, ts), ts)
            value = nt(act_v[rows, :], act_v[core_cols, :])
            if keep:
                s1_keep[k] = value
            else:
                s1_send[k] = value.astype(BF16)

    for k in range(n // 2):
        gelu_part(k)
    step(0, 1)
    for k in range(n // 2, n):
        gelu_part(k)
    step(1, 1)

    s_rows(1 - b, False)
    s1 = pltpu.make_async_remote_copy(
        src_ref=s1_send,
        dst_ref=s1_recv,
        send_sem=s1_sem.at[0],
        recv_sem=s1_sem.at[1],
        device_id=dev(partner),
        device_id_type=MESH,
    )
    s1.start()
    s_rows(b, True)
    w_copy.wait()
    o_own.wait()
    part(0)
    step(0, 2)
    part(1)
    hid_part(0)

    s1.wait()

    @pl.loop(0, A)
    def _(k):
        value = s1_keep[k] + s1_recv[k].astype(F32)
        s1_keep[k] = value
        s2_send[k] = value.astype(BF16)

    s2_copies = []
    for d in range(1, A):
        there = lax.rem(a + d, A)
        copy = pltpu.make_async_remote_copy(
            src_ref=s2_send.at[there],
            dst_ref=s2_recv.at[d - 1],
            send_sem=s2_ssem.at[d - 1],
            recv_sem=s2_rsem.at[d - 1],
            device_id=dev(2 * there + b),
            device_id_type=MESH,
        )
        copy.start()
        s2_copies.append(copy)
    step(1, 2)
    part(2)
    hid_part(1)
    step(0, 3)

    for copy in s2_copies:
        copy.wait()
    total = s1_keep[a]
    for d in range(A - 1):
        total = total + s2_recv[d].astype(F32)
    s_v[core, b, a] = total.astype(BF16)
    s3_copies = []
    for d in range(1, A):
        there = lax.rem(a + d, A)
        copy = pltpu.make_async_remote_copy(
            src_ref=s_v.at[core, b, a],
            dst_ref=s_v.at[core, b, a],
            send_sem=s3_ssem.at[d - 1],
            recv_sem=s3_rsem.at[d - 1],
            device_id=dev(2 * there + b),
            device_id_type=MESH,
        )
        copy.start()
        s3_copies.append(copy)

    @pl.loop(0, hidden // 128)
    def _(c):
        block = pl.ds(pl.multiple_of(c * 128, 128), 128)
        act_t[block, :] = act_v[:, block].T

    act_store = pltpu.make_async_copy(act_t, act_out, local_sem.at[0])
    act_store.start()
    step(1, 3)
    part(3)
    hid_part(2)
    for d in range(1, A):
        copy = s3_copies[d - 1]
        copy.wait_send()
        back = lax.rem(a - d + A, A)
        pltpu.make_async_remote_copy(
            src_ref=s_v.at[core, b, back],
            dst_ref=s_v.at[core, b, back],
            send_sem=s3_ssem.at[d - 1],
            recv_sem=s3_rsem.at[d - 1],
            device_id=dev(2 * back + b),
            device_id_type=MESH,
        ).wait_recv()

    def swap(mine, theirs, sems, device):
        copy = pltpu.make_async_remote_copy(
            src_ref=s_v.at[mine],
            dst_ref=s_v.at[mine],
            send_sem=sems.at[0],
            recv_sem=sems.at[1],
            device_id=device,
            device_id_type=MESH,
        )
        copy.start()
        back = pltpu.make_async_remote_copy(
            src_ref=s_v.at[theirs],
            dst_ref=s_v.at[theirs],
            send_sem=sems.at[0],
            recv_sem=sems.at[1],
            device_id=device,
            device_id_type=MESH,
        )
        return copy, back

    copy, back = swap((core, b), (core, 1 - b), s4_sem, dev(partner))
    for h in range(4, hops):
        step(0, h)
        part(h)
        hid_part(h - 1)
        step(1, h)
    hid_part(hops - 1)
    copy.wait_send()
    back.wait_recv()
    copy, back = swap((core,), (1 - core,), s5_sem, dev(idx, 1 - core))
    step(0, hops)
    o_store = pltpu.make_async_copy(o_v, o_full, local_sem.at[1])
    o_store.start()
    part(hops)
    copy.wait_send()
    back.wait_recv()
    s_store = pltpu.make_async_copy(s_v, s_out, local_sem.at[4])
    s_store.start()
    hid_part(hops)
    step(1, hops)
    for copy in sent:
        copy.wait_send()
    for copy in part_copies:
        copy.wait_send()
    i_own.wait()
    o_store.wait()
    for store in hid_stores:
        store.wait()
    act_store.wait()
    s_store.wait()


def finish(act_t, hid, o, i_tile, own, s, state, down, up, gram, left, keep, state_sem, gram_sem, whole_own=False):
    step = pl.program_id(0)
    rows = keep.shape[0]
    tile = keep.shape[1] // STEPS
    cols = pl.ds(pl.multiple_of(step * tile, tile), tile)
    load = pltpu.make_async_copy(state.at[:, 0, :], keep, state_sem)

    @pl.when(step == 0)
    def _():
        load.start()

    down[...] = nn(act_t[...], o[...]).astype(BF16)
    up[...] = tn(i_tile[...], hid[...]).astype(BF16)

    @pl.when(step == 0)
    def _():
        span = s.shape[2]
        if whole_own:
            mine = own[:, pl.ds(pl.multiple_of(lax.axis_index("inp") * rows, rows), rows)]
        else:
            mine = own[...]
        for c in range(2):
            value = tn(mine, s[c])
            high = value.astype(BF16)
            left[0, :, c * span : (c + 1) * span] = high
            left[1, :, c * span : (c + 1) * span] = (value - high.astype(F32)).astype(BF16)
        load.wait()

    total = nn(left[0], o[:, cols]) + nn(left[1], o[:, cols])
    keep[:, cols] = ema_decay * keep[:, cols] + (1.0 - ema_decay) * total

    def store(k):
        part = pl.ds(k * tile, tile)
        return pltpu.make_async_copy(keep.at[:, part], gram.at[:, 0, part], gram_sem.at[k])

    for k in range(STEPS):

        @pl.when(step == k)
        def _():
            store(k).start()

    @pl.when(step == STEPS - 1)
    def _():
        for k in range(STEPS):
            store(k).wait()


def shards(n, inputs, pre_act, out_grad, w_down, gram_state):
    ts, width = out_grad.shape
    tokens, hidden = pre_act.shape
    A = n // 2
    span = tokens // 2
    hops = n // 2
    shape = jax.ShapeDtypeStruct
    dma = pltpu.SemaphoreType.DMA
    any_spec = pl.BlockSpec(memory_space=pl.ANY)
    vmem_spec = pl.BlockSpec(memory_space=pltpu.VMEM)
    extra = max(A - 1, 1)
    o_full, i_full, hid, act_t, s = pl.pallas_call(
        functools.partial(exchange, n),
        out_shape=(
            shape((tokens, width), BF16),
            shape((tokens, width), BF16),
            shape((tokens, hidden), BF16),
            shape((hidden, tokens), BF16),
            shape((2, 2, A, ts, span), BF16),
        ),
        in_specs=[any_spec, any_spec, vmem_spec, any_spec],
        out_specs=(any_spec,) * 5,
        scratch_shapes=[
            pltpu.VMEM((tokens, width), BF16),
            pltpu.VMEM((tokens, hidden), BF16),
            pltpu.VMEM((tokens, hidden), BF16),
            pltpu.VMEM((hidden, tokens), BF16),
            pltpu.VMEM((hidden, width), BF16),
            pltpu.VMEM((tokens, hidden), F32),
            pltpu.VMEM((tokens, hidden), F32),
            pltpu.VMEM((tokens, hidden), BF16),
            pltpu.VMEM((tokens, hidden), BF16),
            pltpu.VMEM((tokens, hidden), BF16),
            pltpu.VMEM((A, ts, span), F32),
            pltpu.VMEM((A, ts, span), BF16),
            pltpu.VMEM((A, ts, span), BF16),
            pltpu.VMEM((A, ts, span), BF16),
            pltpu.VMEM((extra, ts, span), BF16),
            pltpu.VMEM((2, 2, A, ts, span), BF16),
            dma((2, 2, hops, 2)),
            dma((2, 2, hops, 2)),
            dma((n,)),
            dma((n,)),
            dma((2,)),
            dma((extra,)),
            dma((extra,)),
            dma((extra,)),
            dma((extra,)),
            dma((2,)),
            dma((2,)),
            dma((n,)),
            dma((n,)),
            dma((5,)),
        ],
        compiler_params=pltpu.CompilerParams(
            collective_id=0, has_side_effects=True, vmem_limit_bytes=56 * 1024 * 1024
        ),
        name="exchange",
    )(inputs, pre_act, out_grad, w_down)
    s = s.reshape(2, tokens, span)
    rows = gram_state.shape[0]
    whole_own = rows % 128 == 0
    own = o_full
    if not whole_own:
        own = lax.dynamic_slice_in_dim(o_full, lax.axis_index("inp") * rows, rows, 1)
    fixed = lambda i: (0, 0)
    return pl.pallas_call(
        functools.partial(finish, whole_own=whole_own),
        grid=(STEPS,),
        out_shape=(
            shape((hidden, width), BF16),
            shape((width, hidden), BF16),
            shape(gram_state.shape, F32),
        ),
        in_specs=[
            pl.BlockSpec((hidden // STEPS, tokens), lambda i: (i, 0)),
            pl.BlockSpec((tokens, hidden), fixed),
            pl.BlockSpec((tokens, width), fixed),
            pl.BlockSpec((tokens, width // STEPS), lambda i: (0, i)),
            pl.BlockSpec(own.shape, fixed),
            pl.BlockSpec((2, tokens, span), lambda i: (0, 0, 0)),
            any_spec,
        ],
        out_specs=(
            pl.BlockSpec((hidden // STEPS, width), lambda i: (i, 0)),
            pl.BlockSpec((width // STEPS, hidden), lambda i: (i, 0)),
            any_spec,
        ),
        scratch_shapes=[
            pltpu.VMEM((2, rows, tokens), BF16),
            pltpu.VMEM((rows, width), F32),
            dma(()),
            dma((STEPS,)),
        ],
        compiler_params=pltpu.CompilerParams(vmem_limit_bytes=56 * 1024 * 1024),
        name="finish",
    )(act_t, hid, o_full, i_full, own, s, gram_state)


def solution(mesh):
    return jax.shard_map(
        functools.partial(shards, mesh.shape["inp"]),
        mesh=mesh,
        in_specs=(
            P(("groups", "inp"), "out"),
            P("groups", "inp"),
            P(("groups", "inp"), "out"),
            P("inp", "out"),
            P(("groups", "inp"), "out", None),
        ),
        out_specs=(
            P(("groups", "inp"), "out"),
            P(("groups", "out"), "inp"),
            P(("groups", "inp"), "out", None),
        ),
        check_vma=False,
    )
```
